128 devices in a mesh: expert: 2 (over core), etp: 4 (over x), edp: 16 (over z, y).
Axes of the slice: x: 4, y: 4, z: 4, core: 2. Of those that a mesh axis runs over, the one named last changes fastest.
Arguments:
- expert_ids: int32 [4096, 2], P(('expert', 'edp')), may hold values from 0 to 7, all different within a row; in each aligned block of 128 rows (0 to 127, 128 to 255, ...) at most 64 rows name the same one
- gate_prob: float32 [4096, 2], P(('expert', 'edp')), may hold values from 0.1 to 0.9
- dout: bfloat16 [4096, 6144], P(('expert', 'edp')), may hold values from -6 to 6
- stored_rows: bfloat16 [2, 2048, 6144], P('expert', 'edp'), may hold values from -6 to 6
- w_gate: bfloat16 [2, 6144, 8192], P('expert', 'edp', 'etp'), may hold values from -0.078125 to 0.078125
- w_up: bfloat16 [2, 6144, 8192], P('expert', 'edp', 'etp'), may hold values from -0.078125 to 0.078125
- w_down: bfloat16 [2, 8192, 6144], P('expert', 'etp', 'edp'), may hold values from -0.0625 to 0.0625
Outputs:
- grad_tokens: bfloat16 [4096, 6144], P(('expert', 'edp'), 'etp')
- grad_gate: bfloat16 [2, 6144, 8192], P('expert', 'edp', 'etp')
- grad_up: bfloat16 [2, 6144, 8192], P('expert', 'edp', 'etp')
- grad_down: bfloat16 [2, 8192, 6144], P('expert', 'etp', 'edp')
The draws below stay inside these ranges and needn't reach their ends.
Inputs may be any that keep to these rules, and one draw needn't show every extreme that they name: `expert_ids`: in each block of 128 tokens (the tokens of one owner) no expert is named by more than 64 tokens, a bound that some block reaches; the two ids of a token differ.
All inputs are finite; a program needn't handle non-finite values.
Results may differ from the reference program's by a relative error of at most 0.0058.
Values may be sent and summed in bfloat16 or wider, within the bound.
No kernel may reach another device: no remote copies, remote signals or barrier semaphores. Data moves between devices by JAX's collectives and lax.ppermute only.
A program may use at most 256 MiB of HBM per device.

```python
import math
import jax
import jax.numpy as jnp
import numpy as np

D = 6144
FF = 8192
EXPERTS_ALL = 8
TOK_DEV = 128
CAP = 64
TOKENS = 4096
ROWS_DEV = 128
EXP_ROWS = 2048
N_EXPERT = 2
N_EDP = 16


def levels(key, dims, split, least, largest):
    loudness, own = 1.0, jax.random.fold_in(key, 6)
    for position, blocks in split:
        heights = jnp.exp(jax.random.uniform(jax.random.fold_in(own, position), (blocks,), jnp.float32, least / len(split), largest / len(split)))
        loudness = loudness * jnp.repeat(heights, dims[position] // blocks).reshape([-1 if axis == position else 1 for axis in range(len(dims))])
    return loudness


def deal_out(rng, own, number, rows, number_of, top, most, skew):
    ranking = jax.random.permutation(rng, number_of)
    crowded, common = load_shares(number_of, rows * top, most, skew, True), load_shares(number_of, rows * top, most, skew, False)
    places = jnp.arange(number_of)

    def named(tallies, offset_by):
        used = int((tallies > 0).sum())
        fixed = max(1, used // 4)
        shifted = fixed + (places - fixed + offset_by * (used - fixed)) % max(1, number_of - fixed)
        return jnp.zeros((number_of,), jnp.int32).at[ranking[jnp.where(places < fixed, places, shifted)]].set(jnp.asarray(tallies, jnp.int32))

    tallies = jnp.where(number % 4 == 0, named(crowded, number // 4), named(common, number - number // 4 - 1))
    mixed = jax.random.permutation(jax.random.fold_in(own, 3), number_of)
    donor, taker = mixed[0:number_of // 2 * 2:2], mixed[1:number_of // 2 * 2:2]
    slack = jnp.minimum(tallies[donor] - 1, most - tallies[taker]) // 2
    slack = jnp.where((donor == ranking[0]) | (taker == ranking[0]) | (tallies[taker] == 0), 0, jnp.maximum(slack, 0))
    shifted = jax.random.randint(jax.random.fold_in(own, 4), (number_of // 2,), 0, 1 << 20) % (slack + 1)
    tallies = tallies.at[donor].add(-shifted).at[taker].add(shifted)
    members = jnp.searchsorted(jnp.cumsum(tallies), jnp.arange(rows * top), side="right").astype(jnp.int32)
    table = members.reshape(top, rows).T
    table = table[jax.random.permutation(jax.random.fold_in(own, 1), rows)]
    offset_by = jax.random.randint(jax.random.fold_in(own, 2), (rows, 1), 0, top)
    return jnp.take_along_axis(table, (jnp.arange(top)[None, :] + offset_by) % top, axis=1)


def load_shares(number_of, total, most, slope, full):
    weights = [(1 << 20) // math.isqrt(standing ** slope) + 1 for standing in range(1, number_of + 1)]
    largest = most if full else min(most, max(-(-total // number_of), total * weights[0] // sum(weights)))
    least = 1 if total - largest >= number_of - 1 else 0
    counts, spare = [largest] + [least] * (number_of - 1), total - largest - least * (number_of - 1)
    while spare > 0:
        movable = [i for i in range(1, number_of) if counts[i] < largest] or [i for i in range(1, number_of) if counts[i] < most]
        pool, left = sum([weights[i] for i in movable]), spare
        for i in movable:
            addition = min(most - counts[i], max(1, left * weights[i] // pool), spare)
            counts[i] = counts[i] + addition
            spare = spare - addition
    return np.array(counts)


def gaussian(key, dims, deviation, reach, pieces=(), kind=jnp.bfloat16):
    drawn = jax.random.normal(key, dims, jnp.float32) * deviation
    if len(pieces) > 0:
        drawn = levels(key, dims, pieces, -0.22, 0.18) * drawn
    return jnp.clip(drawn, min=-reach, max=reach).astype(kind)


def setup_inputs(seed: int = 0) -> dict:
    keys = jax.random.split(jax.random.key(seed), 8)
    expert_ids_keys = jax.random.split(jax.random.fold_in(keys[0], 1), TOKENS // TOK_DEV)
    expert_ids_turns = jax.random.permutation(jax.random.fold_in(keys[0], 3), TOKENS // TOK_DEV)
    expert_ids = jax.vmap(lambda own, number: deal_out(jax.random.fold_in(keys[0], 2), own, number, TOK_DEV, EXPERTS_ALL, 2, CAP, 2))(expert_ids_keys, expert_ids_turns).reshape((TOKENS, 2))
    gate_prob = jnp.clip(0.1 + 0.79999997 * jax.random.uniform(keys[1], (TOKENS, 2), jnp.float32) ** levels(keys[1], (TOKENS, 2), ((0, 32),), -0.2, 0.2), 0.1, 0.9)
    dout = gaussian(keys[2], (TOKENS, D), 1.0, 6.0, ((0, 32),))
    stored_rows = gaussian(keys[3], (N_EXPERT, EXP_ROWS, D), 1.0, 6.0, ((0, 2), (1, 16)))
    w_gate = gaussian(keys[4], (N_EXPERT, D, FF), D ** -0.5, 0.078125, ((0, 2), (1, 16), (2, 4)))
    w_up = gaussian(keys[5], (N_EXPERT, D, FF), D ** -0.5, 0.078125, ((0, 2), (1, 16), (2, 4)))
    w_down = gaussian(keys[6], (N_EXPERT, FF, D), FF ** -0.5, 0.0625, ((0, 2), (1, 4), (2, 16)))
    return {"expert_ids": expert_ids, "gate_prob": gate_prob, "dout": dout, "stored_rows": stored_rows, "w_gate": w_gate, "w_up": w_up, "w_down": w_down}


def reference(expert_ids, gate_prob, dout, stored_rows, w_gate, w_up, w_down):
    blocks = N_EXPERT * N_EDP
    id_blocks = expert_ids.reshape(blocks, TOK_DEV, 2)
    prob_blocks = gate_prob.reshape(blocks, TOK_DEV, 2)
    block_index = jnp.arange(blocks, dtype=jnp.int32)
    source = (block_index // N_EDP)[:, None]
    batch = (block_index % N_EDP)[:, None]
    total = jnp.zeros((TOKENS, D), jnp.float32)
    grads_gate = []
    grads_up = []
    grads_down = []
    for expert in range(N_EXPERT):
        named = id_blocks == expert
        chosen = jnp.any(named, axis=2)
        weight_row = jnp.sum(jnp.where(named, prob_blocks, jnp.float32(0.0)), axis=2)
        rank = jnp.cumsum(chosen.astype(jnp.int32), axis=1) - 1
        row_index = batch * ROWS_DEV + source * CAP + rank
        row_index = jnp.where(chosen, row_index, EXP_ROWS).astype(jnp.int32).reshape(-1)
        scaled = (weight_row.reshape(-1, 1) * dout.astype(jnp.float32)).astype(jnp.bfloat16)
        holder = jnp.zeros((EXP_ROWS + 1, D), jnp.float32).at[row_index].add(scaled.astype(jnp.float32))
        dispatched = holder[:EXP_ROWS].astype(jnp.bfloat16)
        inputs = stored_rows[expert]
        gate = jnp.dot(inputs, w_gate[expert], preferred_element_type=jnp.float32)
        up_val = jnp.dot(inputs, w_up[expert], preferred_element_type=jnp.float32)
        dhidden = jnp.dot(dispatched, w_down[expert].T, preferred_element_type=jnp.float32)
        sig = jax.nn.sigmoid(gate)
        act = gate * sig
        hidden = (act * up_val).astype(jnp.bfloat16)
        dup = (dhidden * act).astype(jnp.bfloat16)
        dgate = (dhidden * up_val * sig * (1.0 + gate * (1.0 - sig))).astype(jnp.bfloat16)
        grads_gate.append(jnp.dot(inputs.T, dgate, preferred_element_type=jnp.float32).astype(jnp.bfloat16))
        grads_up.append(jnp.dot(inputs.T, dup, preferred_element_type=jnp.float32).astype(jnp.bfloat16))
        grads_down.append(jnp.dot(hidden.T, dispatched, preferred_element_type=jnp.float32).astype(jnp.bfloat16))
        drows = jnp.dot(dgate, w_gate[expert].T, preferred_element_type=jnp.float32)
        drows = drows + jnp.dot(dup, w_up[expert].T, preferred_element_type=jnp.float32)
        padded = jnp.concatenate([drows.astype(jnp.bfloat16), jnp.zeros((1, D), jnp.bfloat16)], axis=0)
        total = total + jnp.take(padded, row_index, axis=0).astype(jnp.float32)
    return (total.astype(jnp.bfloat16), jnp.stack(grads_gate), jnp.stack(grads_up), jnp.stack(grads_down))
```

```python
import jax
import jax.numpy as jnp
from jax import lax
from jax.sharding import Mesh
from jax.sharding import PartitionSpec as P

BF16 = jnp.bfloat16
F32 = jnp.float32
RING = 4


def hop(value, axis, step):
    return lax.ppermute(value, axis, [(i, (i + step) % RING) for i in range(RING)])


def ring_gather(block, axis):
    half = block.shape[0] // 2
    below = hop(block, axis, 1)
    above = hop(block, axis, -1)
    far_low = hop(below[:half], axis, 1)
    far_high = hop(above[half:], axis, -1)
    return [block, above, jnp.concatenate([far_low, far_high]), below]


def ring_scatter(parts, axis):
    half = parts[2].shape[0] // 2
    far = parts[2].astype(BF16)
    from_below = hop(far[:half], axis, 1).astype(F32)
    from_above = hop(far[half:], axis, -1).astype(F32)
    up = jnp.concatenate([parts[1][:half] + from_below, parts[1][half:]]).astype(BF16)
    down = jnp.concatenate([parts[3][:half], parts[3][half:] + from_above]).astype(BF16)
    return parts[0] + hop(up, axis, 1).astype(F32) + hop(down, axis, -1).astype(F32)


def exchange(blocks, axis):
    return [blocks[0], hop(blocks[3], axis, -1), hop(blocks[2], axis, 2), hop(blocks[1], axis, 1)]


def cut(value, dim, place, size):
    return lax.dynamic_slice_in_dim(value, place * size, size, dim)


def laid(blocks, dim, me):
    size = blocks[0].shape[dim]
    shape = list(blocks[0].shape)
    shape[dim] = size * RING
    whole = jnp.zeros(shape, blocks[0].dtype)
    for k, block in enumerate(blocks):
        whole = lax.dynamic_update_slice_in_dim(whole, block, (me + k) % RING * size, dim)
    return whole


def dot(a, b, dims):
    return lax.dot_general(a, b, (dims, ((), ())), preferred_element_type=F32)


def local(expert_ids, gate_prob, dout, stored_rows, w_gate, w_up, w_down):
    x, y, z = lax.axis_index("etp"), lax.axis_index("y"), lax.axis_index("z")
    owners = 2
    tokens = dout.shape[0]
    width = dout.shape[1]
    rows = stored_rows.shape[1]
    capacity = rows // owners
    quarter = capacity // RING
    features = width // RING
    hidden_width = w_gate.shape[2]
    block_ff = hidden_width // RING
    block_d = w_gate.shape[1]

    def to_features(part):
        return jnp.concatenate(exchange([cut(part, 1, (z + k) % RING, features) for k in range(RING)], "z"))

    def to_all_rows(part):
        along_y = jnp.concatenate(ring_gather(to_features(part), "y"))
        return jnp.concatenate(ring_gather(along_y, "etp"))

    mine = stored_rows[0].reshape(owners, RING, quarter, width)
    mine = lax.dynamic_index_in_dim(mine, x, 1, keepdims=False).reshape(owners * quarter, width)
    x_all = to_all_rows(mine)

    gate_up = [
        jnp.concatenate([cut(w[0], 1, (y + k) % RING, block_ff) for w in (w_gate, w_up)], axis=1) for k in range(RING)
    ]
    gate_up = laid(exchange(gate_up, "y"), 0, y)
    down = laid(exchange([cut(w_down[0], 0, (y + k) % RING, block_ff) for k in range(RING)], "y"), 1, y)

    slots = lax.broadcasted_iota(jnp.int32, (capacity, tokens), 0)
    placings = []
    outgoing = []
    for expert in range(owners):
        named = expert_ids == expert
        chosen = jnp.any(named, axis=1)
        weight_row = jnp.sum(jnp.where(named, gate_prob, jnp.float32(0.0)), axis=1)
        rank = jnp.cumsum(chosen.astype(jnp.int32)) - 1
        placing = (chosen[None, :] & (rank[None, :] == slots)).astype(BF16)
        scaled = (weight_row[:, None] * dout.astype(F32)).astype(BF16)
        outgoing.append(dot(cut(placing, 0, x, quarter), scaled, ((1,), (0,))).astype(BF16))
        placings.append(placing)
    incoming = lax.all_to_all(jnp.stack(outgoing), "expert", split_axis=0, concat_axis=0, tiled=True)
    dy_all = to_all_rows(incoming.reshape(owners * quarter, width))

    def over_features(product):
        parts = product.reshape(RING * RING, RING, owners * quarter, -1)
        return ring_scatter([parts[:, k].reshape(-1, parts.shape[-1]) for k in range(RING)], "z")

    def of_all_rows(own):
        blocks = jnp.stack(ring_gather(own, "z")).reshape(RING, RING * RING, owners * quarter, -1)
        return blocks.transpose(1, 0, 2, 3).reshape(-1, own.shape[1])

    gate_up_own = over_features(dot(x_all, gate_up, ((1,), (0,))))
    dhidden = over_features(dot(dy_all, down, ((1,), (1,))))
    gate, up = gate_up_own[:, :block_ff], gate_up_own[:, block_ff:]
    sig = jax.nn.sigmoid(gate)
    act = gate * sig
    hidden = (act * up).astype(BF16)
    dup = (dhidden * act).astype(BF16)
    dgate = (dhidden * up * sig * (1.0 + gate * (1.0 - sig))).astype(BF16)
    hidden_all = of_all_rows(hidden)
    d_all = of_all_rows(jnp.concatenate([dgate, dup], axis=1))

    dx = dot(d_all, gate_up, ((1,), (1,)))
    count = dx.shape[0] // RING
    dx = ring_scatter([dx[k * count : (k + 1) * count] for k in range(RING)], "etp")
    count = count // RING
    dx = ring_scatter([dx[k * count : (k + 1) * count] for k in range(RING)], "y").astype(BF16)
    count = count // RING
    dx = laid(exchange([dx[k * count : (k + 1) * count] for k in range(RING)], "z"), 1, z)
    back = exchange([cut(dx, 1, (x + k) % RING, features) for k in range(RING)], "etp")
    back = laid([b.reshape(owners, 1, quarter, features) for b in back], 1, x).reshape(owners, capacity, features)
    returned = lax.all_to_all(back, "expert", split_axis=0, concat_axis=0, tiled=True)
    grad_tokens = jnp.einsum("esj,esd->jd", jnp.stack(placings), returned, preferred_element_type=F32)

    grad_down = dot(hidden_all, dy_all, ((0,), (0,))).astype(BF16)
    grad_down = laid(exchange([cut(grad_down, 1, (y + k) % RING, block_d) for k in range(RING)], "y"), 0, y)
    grads = dot(x_all, d_all, ((0,), (0,))).astype(BF16)
    grads = exchange([cut(grads, 0, (y + k) % RING, block_d) for k in range(RING)], "y")
    grad_gate = laid([g[:, :block_ff] for g in grads], 1, y)
    grad_up = laid([g[:, block_ff:] for g in grads], 1, y)
    return grad_tokens.astype(BF16), grad_gate[None], grad_up[None], grad_down[None]


def solution(mesh):
    owners, ring, batches = (mesh.shape[name] for name in ("expert", "etp", "edp"))
    grid = Mesh(mesh.devices.reshape(owners, ring, RING, batches // RING), ("expert", "etp", "z", "y"))
    tokens = ("expert", "z", "y")
    batch = ("z", "y")
    in_specs = (
        P(tokens, None),
        P(tokens, None),
        P(tokens, None),
        P("expert", batch, None),
        P("expert", batch, "etp"),
        P("expert", batch, "etp"),
        P("expert", "etp", batch),
    )
    out_specs = (
        P(tokens, "etp"),
        P("expert", batch, "etp"),
        P("expert", batch, "etp"),
        P("expert", "etp", batch),
    )
    return jax.shard_map(local, mesh=grid, in_specs=in_specs, out_specs=out_specs, check_vma=False)
```

```python
import jax
import jax.numpy as jnp
from jax import lax
from jax.sharding import Mesh
from jax.sharding import PartitionSpec as P

BF16 = jnp.bfloat16
F32 = jnp.float32
RING = 4
DEVICES = ("expert", "etp", "z", "y")
ROLES = {"x": ("etp", "etp"), "b": ("y", "z"), "c": ("z", "y"), "near": ("y", "etp"), "far": ("etp", "z")}


def hop(value, role, step):
    pairs = []
    for core, axis in enumerate(ROLES[role]):
        for place in range(RING**3):
            at = {"etp": place // RING**2, "z": place // RING % RING, "y": place % RING}
            at[axis] = (at[axis] + step) % RING
            target = (at["etp"] * RING + at["z"]) * RING + at["y"]
            pairs.append((core * RING**3 + place, core * RING**3 + target))
    return lax.ppermute(value, DEVICES, pairs)


def position(role):
    first, second = (lax.axis_index(axis) for axis in ROLES[role])
    return jnp.where(lax.axis_index("expert") == 0, first, second)


def exchange(blocks, role):
    return [blocks[0], hop(blocks[3], role, -1), hop(blocks[2], role, 2), hop(blocks[1], role, 1)]


def ring_exchange(blocks, role):
    half = blocks[2].shape[0] // 2
    up = hop(jnp.concatenate([blocks[1], blocks[2][:half]]), role, 1)
    down = hop(jnp.concatenate([blocks[3], blocks[2][half:]]), role, -1)
    far = jnp.concatenate([hop(up[2 * half :], role, 1), hop(down[2 * half :], role, -1)])
    return [blocks[0], down[: 2 * half], far, up[: 2 * half]]


def gather(block, role):
    return exchange([block] * RING, role)


def scatter(parts, role):
    arrived = exchange([parts[0]] + [p.astype(BF16) for p in parts[1:]], role)
    return arrived[0] + arrived[1].astype(F32) + arrived[2].astype(F32) + arrived[3].astype(F32)


def ring_gather(block, role):
    half = block.shape[0] // 2
    below = hop(block, role, 1)
    above = hop(block, role, -1)
    far_low = hop(below[:half], role, 1)
    far_high = hop(above[half:], role, -1)
    return [block, above, jnp.concatenate([far_low, far_high]), below]


def ring_scatter(parts, role):
    half = parts[2].shape[0] // 2
    far = parts[2].astype(BF16)
    from_below = hop(far[:half], role, 1)
    from_above = hop(far[half:], role, -1)
    up = jnp.concatenate([parts[1][:half] + from_below.astype(F32), parts[1][half:]]).astype(BF16)
    down = jnp.concatenate([parts[3][:half], parts[3][half:] + from_above.astype(F32)]).astype(BF16)
    total = parts[0] + hop(up, role, 1).astype(F32) + hop(down, role, -1).astype(F32)
    return total, (from_below, from_above)


def cut(value, dim, place, size):
    return lax.dynamic_slice_in_dim(value, place % RING * size, size, dim)


def laid(blocks, dim, me):
    size = blocks[0].shape[dim]
    shape = list(blocks[0].shape)
    shape[dim] = size * RING
    whole = jnp.zeros(shape, blocks[0].dtype)
    for k, block in enumerate(blocks):
        whole = lax.dynamic_update_slice_in_dim(whole, block, (me + k) % RING * size, dim)
    return whole


def rows_of(value, count):
    return [value[k * count : (k + 1) * count] for k in range(RING)]


def after(value, *others):
    return lax.optimization_barrier((value, *others))[0]


def dot(a, b, dims):
    return lax.dot_general(a, b, (dims, ((), ())), preferred_element_type=F32)


def reordered(value, core):
    split = value.reshape(value.shape[0], RING, RING, -1)
    return jnp.where(core == 0, split, split.transpose(0, 2, 1, 3)).reshape(value.shape)


def local(expert_ids, gate_prob, dout, stored_rows, w_gate, w_up, w_down):
    core, x, b, c = lax.axis_index("expert"), position("x"), position("b"), position("c")
    owners = 2
    tokens, width = dout.shape
    rows = stored_rows.shape[1]
    capacity = rows // owners
    quarter = capacity // RING
    features = width // RING
    block_ff = w_gate.shape[2] // RING
    block_d = w_gate.shape[1]

    def to_features(part):
        part = reordered(part, core)
        return jnp.concatenate(exchange([cut(part, 1, c + k, features) for k in range(RING)], "c"))

    mine = stored_rows[0].reshape(owners, RING, quarter, width)
    mine = lax.dynamic_index_in_dim(mine, x, 1, keepdims=False).reshape(owners * quarter, width)
    x_mine = to_features(mine)
    x_near = jnp.concatenate(gather(x_mine, "near"))
    dout = after(dout, x_mine)

    slots = lax.broadcasted_iota(jnp.int32, (capacity, tokens), 0)
    placings = []
    outgoing = []
    for expert in range(owners):
        named = expert_ids == expert
        chosen = jnp.any(named, axis=1)
        weight_row = jnp.sum(jnp.where(named, gate_prob, jnp.float32(0.0)), axis=1)
        rank = jnp.cumsum(chosen.astype(jnp.int32)) - 1
        placing = (chosen[None, :] & (rank[None, :] == slots)).astype(BF16)
        scaled = (weight_row[:, None] * dout.astype(F32)).astype(BF16)
        outgoing.append(dot(cut(placing, 0, x, quarter), scaled, ((1,), (0,))).astype(BF16))
        placings.append(placing)
    incoming = lax.all_to_all(jnp.stack(outgoing), "expert", split_axis=0, concat_axis=0, tiled=True)
    weights = jnp.concatenate([w_gate[0], w_up[0], w_down[0].T], axis=1).reshape(block_d, 3, RING, block_ff)
    weights = after(weights, x_mine)
    blocks = [lax.dynamic_index_in_dim(weights, (b + k) % RING, 2, keepdims=False) for k in range(RING)]
    weights = exchange([block.reshape(block_d, -1) for block in blocks], "b")
    dy_mine = to_features(after(incoming, x_near).reshape(owners * quarter, width))
    x_all = ring_gather(x_near, "far")
    dy_near = jnp.concatenate(gather(after(dy_mine, x_all[1], x_all[3]), "far"))
    x_all = jnp.concatenate(x_all)
    weights = laid(weights, 0, b)
    gate_up, down = weights[:, : 2 * block_ff], weights[:, 2 * block_ff :]
    dy_all = jnp.concatenate(ring_gather(dy_near, "near"))

    def over_features(product):
        parts = product.reshape(RING * RING, RING, owners * quarter, -1)
        return scatter([parts[:, k].reshape(-1, parts.shape[-1]) for k in range(RING)], "c")

    def of_all_rows(gathered):
        blocks = jnp.stack(gathered).reshape(RING, RING * RING, owners * quarter, -1)
        return blocks.transpose(1, 0, 2, 3).reshape(-1, blocks.shape[-1])

    def turned(own):
        return own.reshape(RING, RING, owners * quarter, -1).swapaxes(0, 1).reshape(own.shape)

    gate_up_own = over_features(dot(x_all, gate_up, ((1,), (0,))))
    gate, up = gate_up_own[:, :block_ff], gate_up_own[:, block_ff:]
    sig = jax.nn.sigmoid(gate)
    act = gate * sig
    hidden = (act * up).astype(BF16)
    dhidden = turned(over_features(dot(dy_all, down, ((1,), (0,)))))
    dup = (dhidden * act).astype(BF16)
    dgate = (dhidden * up * sig * (1.0 + gate * (1.0 - sig))).astype(BF16)
    both = gather(jnp.concatenate([dgate, dup], axis=1), "c")
    d_all = of_all_rows(both)

    count = d_all.shape[0] // RING
    dx = [dot(part, gate_up, ((1,), (1,))) for part in rows_of(d_all, count)]
    dx, arrived = ring_scatter(dx, "far")
    grads = dot(after(x_all, *arrived), d_all, ((0,), (0,))).astype(BF16)
    count = count // RING
    hidden_all = of_all_rows(gather(after(turned(hidden), *both[1:]), "c"))
    grad_down = after(dot(hidden_all, dy_all, ((0,), (0,))).astype(BF16), *arrived)
    grad_down = exchange([cut(grad_down, 1, b + k, block_d) for k in range(RING)], "b")
    grads = after(grads, dx)
    grads = ring_exchange([cut(grads, 0, b + k, block_d) for k in range(RING)], "b")
    dx = scatter(rows_of(after(dx, *grad_down[1:]), count), "near").astype(BF16)
    dx = reordered(laid(exchange(rows_of(dx, count // RING), "c"), 1, c), core)
    back = exchange([cut(dx, 1, x + k, features) for k in range(RING)], "x")
    back = laid([p.reshape(owners, 1, quarter, features) for p in back], 1, x).reshape(owners, capacity, features)
    returned = lax.all_to_all(after(back, *grads[1:]), "expert", split_axis=0, concat_axis=0, tiled=True)
    grad_tokens = jnp.einsum("esj,esd->jd", jnp.stack(placings), returned, preferred_element_type=F32)

    grad_down = laid(grad_down, 0, b)
    grad_gate = laid([g[:, :block_ff] for g in grads], 1, b)
    grad_up = laid([g[:, block_ff:] for g in grads], 1, b)
    return grad_tokens.astype(BF16), grad_gate[None], grad_up[None], grad_down[None]


def solution(mesh):
    owners, ring, batches = (mesh.shape[name] for name in ("expert", "etp", "edp"))
    grid = Mesh(mesh.devices.reshape(owners, ring, RING, batches // RING), DEVICES)
    tokens = ("expert", "z", "y")
    batch = ("z", "y")
    in_specs = (
        P(tokens, None),
        P(tokens, None),
        P(tokens, None),
        P("expert", batch, None),
        P("expert", batch, "etp"),
        P("expert", batch, "etp"),
        P("expert", "etp", batch),
    )
    out_specs = (
        P(tokens, "etp"),
        P("expert", batch, "etp"),
        P("expert", batch, "etp"),
        P("expert", "etp", batch),
    )
    return jax.shard_map(local, mesh=grid, in_specs=in_specs, out_specs=out_specs, check_vma=False)
```

```python
import jax
import jax.numpy as jnp
from jax import lax
from jax.sharding import Mesh
from jax.sharding import PartitionSpec as P

BF16 = jnp.bfloat16
F32 = jnp.float32
RING = 4
DEVICES = ("expert", "etp", "z", "y")
ROLES = {"x": ("etp", "etp"), "b": ("y", "z"), "c": ("z", "y"), "near": ("y", "etp"), "far": ("etp", "z")}


def hop(value, role, step):
    pairs = []
    for core, axis in enumerate(ROLES[role]):
        for place in range(RING**3):
            at = {"etp": place // RING**2, "z": place // RING % RING, "y": place % RING}
            at[axis] = (at[axis] + step) % RING
            target = (at["etp"] * RING + at["z"]) * RING + at["y"]
            pairs.append((core * RING**3 + place, core * RING**3 + target))
    return lax.ppermute(value, DEVICES, pairs)


def position(role):
    first, second = (lax.axis_index(axis) for axis in ROLES[role])
    return jnp.where(lax.axis_index("expert") == 0, first, second)


def beside(blocks, role):
    return hop(blocks[3], role, -1), hop(blocks[1], role, 1)


def across(blocks, role):
    return hop(blocks[2], role, 2)


def exchange(blocks, role):
    above, below = beside(blocks, role)
    return [blocks[0], above, across(blocks, role), below]


def gather(block, role):
    return exchange([block] * RING, role)


def scatter(parts, role):
    arrived = exchange([parts[0]] + [p.astype(BF16) for p in parts[1:]], role)
    return arrived[0] + arrived[1].astype(F32) + arrived[2].astype(F32) + arrived[3].astype(F32)


def far_first(block, role):
    return hop(block, role, -1), hop(block, role, 1)


def far_second(above, below, role):
    half = above.shape[0] // 2
    return hop(below[:half], role, 1), hop(above[half:], role, -1)


def ring_scatter(parts, role):
    half = parts[2].shape[0] // 2
    far = parts[2].astype(BF16)
    from_below = hop(far[:half], role, 1)
    from_above = hop(far[half:], role, -1)
    up = jnp.concatenate([parts[1][:half] + from_below.astype(F32), parts[1][half:]]).astype(BF16)
    down = jnp.concatenate([parts[3][:half], parts[3][half:] + from_above.astype(F32)]).astype(BF16)
    total = parts[0] + hop(up, role, 1).astype(F32) + hop(down, role, -1).astype(F32)
    return total, (from_below, from_above)


def cut(value, dim, place, size):
    return lax.dynamic_slice_in_dim(value, place % RING * size, size, dim)


def laid(blocks, dim, me):
    size = blocks[0].shape[dim]
    shape = list(blocks[0].shape)
    shape[dim] = size * RING
    whole = jnp.zeros(shape, blocks[0].dtype)
    for k, block in enumerate(blocks):
        whole = lax.dynamic_update_slice_in_dim(whole, block, (me + k) % RING * size, dim)
    return whole


def rows_of(value, count):
    return [value[k * count : (k + 1) * count] for k in range(RING)]


def after(value, *others):
    return lax.optimization_barrier((value, *others))[0]


def dot(a, b, dims):
    return lax.dot_general(a, b, (dims, ((), ())), preferred_element_type=F32)


def reordered(value, core):
    split = value.reshape(value.shape[0], RING, RING, -1)
    return jnp.where(core == 0, split, split.transpose(0, 2, 1, 3)).reshape(value.shape)


def local(expert_ids, gate_prob, dout, stored_rows, w_gate, w_up, w_down):
    core, x, b, c = lax.axis_index("expert"), position("x"), position("b"), position("c")
    owners = 2
    tokens, width = dout.shape
    rows = stored_rows.shape[1]
    capacity = rows // owners
    quarter = capacity // RING
    features = width // RING
    block_ff = w_gate.shape[2] // RING
    block_d = w_gate.shape[1]

    def to_features(part):
        part = reordered(part, core)
        return jnp.concatenate(exchange([cut(part, 1, c + k, features) for k in range(RING)], "c"))

    mine = stored_rows[0].reshape(owners, RING, quarter, width)
    mine = lax.dynamic_index_in_dim(mine, x, 1, keepdims=False).reshape(owners * quarter, width)
    x_mine = to_features(mine)
    x_near = jnp.concatenate(gather(x_mine, "near"))
    dout, expert_ids = after(dout, x_mine), after(expert_ids, x_mine)

    slots = lax.broadcasted_iota(jnp.int32, (capacity, tokens), 0)
    placings = []
    outgoing = []
    for expert in range(owners):
        named = expert_ids == expert
        chosen = jnp.any(named, axis=1)
        weight_row = jnp.sum(jnp.where(named, gate_prob, jnp.float32(0.0)), axis=1)
        rank = jnp.cumsum(chosen.astype(jnp.int32)) - 1
        placing = (chosen[None, :] & (rank[None, :] == slots)).astype(BF16)
        scaled = (weight_row[:, None] * dout.astype(F32)).astype(BF16)
        outgoing.append(dot(cut(placing, 0, x, quarter), scaled, ((1,), (0,))).astype(BF16))
        placings.append(placing)
    incoming = lax.all_to_all(jnp.stack(outgoing), "expert", split_axis=0, concat_axis=0, tiled=True)
    weights = jnp.concatenate([w_gate[0], w_up[0], w_down[0].T], axis=1).reshape(block_d, 3, RING, block_ff)
    weights = after(weights, x_mine)
    blocks = [lax.dynamic_index_in_dim(weights, (b + k) % RING, 2, keepdims=False) for k in range(RING)]
    blocks = [block.reshape(block_d, -1) for block in blocks]
    weights = exchange(blocks, "b")
    dy_mine = to_features(after(incoming, x_near).reshape(owners * quarter, width))
    beside_x = far_first(x_near, "far")
    across_x = far_second(*beside_x, "far")
    dy_near = jnp.concatenate(gather(after(dy_mine, *beside_x), "far"))
    beside_dy = far_first(dy_near, "near")
    weights = lax.optimization_barrier((*weights, dy_near))[:RING]
    x_all = jnp.concatenate([x_near, beside_x[0], *across_x, beside_x[1]])
    weights = laid(weights, 0, b)
    gate_up, down = weights[:, : 2 * block_ff], weights[:, 2 * block_ff :]
    product = dot(x_all, gate_up, ((1,), (0,)))
    beside_dy, product = lax.optimization_barrier((beside_dy, product))
    across_dy = far_second(*beside_dy, "near")
    dy_all = jnp.concatenate([dy_near, beside_dy[0], *across_dy, beside_dy[1]])

    def over_features(product):
        parts = product.reshape(RING * RING, RING, owners * quarter, -1)
        return scatter([parts[:, k].reshape(-1, parts.shape[-1]) for k in range(RING)], "c")

    def of_all_rows(gathered):
        blocks = jnp.stack(gathered).reshape(RING, RING * RING, owners * quarter, -1)
        return blocks.transpose(1, 0, 2, 3).reshape(-1, blocks.shape[-1])

    def turned(own):
        return own.reshape(RING, RING, owners * quarter, -1).swapaxes(0, 1).reshape(own.shape)

    gate_up_own = over_features(product)
    gate, up = gate_up_own[:, :block_ff], gate_up_own[:, block_ff:]
    sig = jax.nn.sigmoid(gate)
    act = gate * sig
    hidden = (act * up).astype(BF16)
    dhidden = turned(over_features(dot(dy_all, down, ((1,), (0,)))))
    dup = (dhidden * act).astype(BF16)
    dgate = (dhidden * up * sig * (1.0 + gate * (1.0 - sig))).astype(BF16)
    both = gather(jnp.concatenate([dgate, dup], axis=1), "c")
    d_all = of_all_rows(both)

    count = d_all.shape[0] // RING
    dx = [dot(part, gate_up, ((1,), (1,))) for part in rows_of(d_all, count)]
    dx, arrived = ring_scatter(dx, "far")
    grads = dot(after(x_all, *arrived), d_all, ((0,), (0,))).astype(BF16)
    count = count // RING
    hidden_all = of_all_rows(gather(after(turned(hidden), *both[1:]), "c"))
    grad_down = after(dot(hidden_all, dy_all, ((0,), (0,))).astype(BF16), *arrived)
    grad_down = exchange([cut(grad_down, 1, b + k, block_d) for k in range(RING)], "b")
    grads = after(grads, *grad_down[1:])
    grads = [cut(grads, 0, b + k, block_d) for k in range(RING)]
    half = block_d // 2
    up = hop(jnp.concatenate([grads[1], grads[2][:half]]), "b", 1)
    low = hop(jnp.concatenate([grads[3], grads[2][half:]]), "b", -1)
    opposite = jnp.concatenate([hop(up[block_d:], "b", 1), hop(low[block_d:], "b", -1)])
    grads = [grads[0], low[:block_d], opposite, up[:block_d]]
    dx = scatter(rows_of(dx, count), "near").astype(BF16)
    dx = reordered(laid(exchange(rows_of(dx, count // RING), "c"), 1, c), core)
    back = exchange([cut(dx, 1, x + k, features) for k in range(RING)], "x")
    back = laid([p.reshape(owners, 1, quarter, features) for p in back], 1, x).reshape(owners, capacity, features)
    returned = lax.all_to_all(after(back, *grads[1:]), "expert", split_axis=0, concat_axis=0, tiled=True)
    grad_tokens = jnp.einsum("esj,esd->jd", jnp.stack(placings), returned, preferred_element_type=F32)

    grad_down = laid(grad_down, 0, b)
    grad_gate = laid([g[:, :block_ff] for g in grads], 1, b)
    grad_up = laid([g[:, block_ff:] for g in grads], 1, b)
    return grad_tokens.astype(BF16), grad_gate[None], grad_up[None], grad_down[None]


def solution(mesh):
    owners, ring, batches = (mesh.shape[name] for name in ("expert", "etp", "edp"))
    grid = Mesh(mesh.devices.reshape(owners, ring, RING, batches // RING), DEVICES)
    tokens = ("expert", "z", "y")
    batch = ("z", "y")
    in_specs = (
        P(tokens, None),
        P(tokens, None),
        P(tokens, None),
        P("expert", batch, None),
        P("expert", batch, "etp"),
        P("expert", batch, "etp"),
        P("expert", "etp", batch),
    )
    out_specs = (
        P(tokens, "etp"),
        P("expert", batch, "etp"),
        P("expert", batch, "etp"),
        P("expert", "etp", batch),
    )
    return jax.shard_map(local, mesh=grid, in_specs=in_specs, out_specs=out_specs, check_vma=False)
```

```python
import jax
import jax.numpy as jnp
from jax import lax
from jax.sharding import Mesh
from jax.sharding import PartitionSpec as P

BF16 = jnp.bfloat16
F32 = jnp.float32
RING = 4
DEVICES = ("expert", "etp", "z", "y")
ROLES = {"x": ("etp", "etp"), "b": ("y", "z"), "c": ("z", "y"), "near": ("y", "etp"), "far": ("etp", "z")}


def hop(value, role, step):
    pairs = []
    for core, axis in enumerate(ROLES[role]):
        for place in range(RING**3):
            at = {"etp": place // RING**2, "z": place // RING % RING, "y": place % RING}
            at[axis] = (at[axis] + step) % RING
            target = (at["etp"] * RING + at["z"]) * RING + at["y"]
            pairs.append((core * RING**3 + place, core * RING**3 + target))
    return lax.ppermute(value, DEVICES, pairs)


def position(role):
    first, second = (lax.axis_index(axis) for axis in ROLES[role])
    return jnp.where(lax.axis_index("expert") == 0, first, second)


def beside(blocks, role):
    return hop(blocks[3], role, -1), hop(blocks[1], role, 1)


def across(blocks, role):
    return hop(blocks[2], role, 2)


def exchange(blocks, role):
    above, below = beside(blocks, role)
    return [blocks[0], above, across(blocks, role), below]


def gather(block, role):
    return exchange([block] * RING, role)


def scatter(parts, role):
    arrived = exchange([parts[0]] + [p.astype(BF16) for p in parts[1:]], role)
    return arrived[0] + arrived[1].astype(F32) + arrived[2].astype(F32) + arrived[3].astype(F32)


def far_first(block, role):
    return hop(block, role, -1), hop(block, role, 1)


def far_second(above, below, role):
    half = above.shape[0] // 2
    return hop(below[:half], role, 1), hop(above[half:], role, -1)


def ring_scatter(parts, role):
    half = parts[2].shape[0] // 2
    far = parts[2].astype(BF16)
    from_below = hop(far[:half], role, 1)
    from_above = hop(far[half:], role, -1)
    up = jnp.concatenate([parts[1][:half] + from_below.astype(F32), parts[1][half:]]).astype(BF16)
    down = jnp.concatenate([parts[3][:half], parts[3][half:] + from_above.astype(F32)]).astype(BF16)
    total = parts[0] + hop(up, role, 1).astype(F32) + hop(down, role, -1).astype(F32)
    return total, (from_below, from_above)


def cut(value, dim, place, size):
    return lax.dynamic_slice_in_dim(value, place % RING * size, size, dim)


def laid(blocks, dim, me):
    size = blocks[0].shape[dim]
    shape = list(blocks[0].shape)
    shape[dim] = size * RING
    whole = jnp.zeros(shape, blocks[0].dtype)
    for k, block in enumerate(blocks):
        whole = lax.dynamic_update_slice_in_dim(whole, block, (me + k) % RING * size, dim)
    return whole


def rows_of(value, count):
    return [value[k * count : (k + 1) * count] for k in range(RING)]


def after(value, *others):
    return lax.optimization_barrier((value, *others))[0]


def dot(a, b, dims):
    return lax.dot_general(a, b, (dims, ((), ())), preferred_element_type=F32)


def local(expert_ids, gate_prob, dout, stored_rows, w_gate, w_up, w_down):
    core, x, b, c = lax.axis_index("expert"), position("x"), position("b"), position("c")
    owners = 2
    tokens, width = dout.shape
    rows = stored_rows.shape[1]
    capacity = rows // owners
    quarter = capacity // RING
    features = width // RING
    block_ff = w_gate.shape[2] // RING
    block_d = w_gate.shape[1]

    def to_features(part):
        blocks = []
        for k in range(RING):
            place = (c + k) % RING
            starts = [jnp.where(core == 0, RING * place + j, RING * j + place) * block_d for j in range(RING)]
            blocks.append(jnp.concatenate([lax.dynamic_slice_in_dim(part, s, block_d, 1) for s in starts], axis=1))
        return jnp.concatenate(exchange(blocks, "c"))

    mine = stored_rows[0].reshape(owners, RING, quarter, width)
    mine = lax.dynamic_index_in_dim(mine, x, 1, keepdims=False).reshape(owners * quarter, width)
    x_mine = to_features(mine)
    x_near = jnp.concatenate(gather(x_mine, "near"))
    dout, expert_ids = after(dout, x_mine), after(expert_ids, x_mine)

    slots = lax.broadcasted_iota(jnp.int32, (capacity, tokens), 0)
    placings = []
    outgoing = []
    for expert in range(owners):
        named = expert_ids == expert
        chosen = jnp.any(named, axis=1)
        weight_row = jnp.sum(jnp.where(named, gate_prob, jnp.float32(0.0)), axis=1)
        rank = jnp.cumsum(chosen.astype(jnp.int32)) - 1
        placing = (chosen[None, :] & (rank[None, :] == slots)).astype(BF16)
        scaled = (weight_row[:, None] * dout.astype(F32)).astype(BF16)
        outgoing.append(dot(cut(placing, 0, x, quarter), scaled, ((1,), (0,))).astype(BF16))
        placings.append(placing)
    incoming = lax.all_to_all(jnp.stack(outgoing), "expert", split_axis=0, concat_axis=0, tiled=True)
    weights = jnp.concatenate([w_gate[0], w_up[0], w_down[0].T], axis=1).reshape(block_d, 3, RING, block_ff)
    weights = after(weights, x_mine)
    blocks = [lax.dynamic_index_in_dim(weights, (b + k) % RING, 2, keepdims=False) for k in range(RING)]
    blocks = [block.reshape(block_d, -1) for block in blocks]
    weights = exchange(blocks, "b")
    dy_mine = to_features(after(incoming, x_near).reshape(owners * quarter, width))
    beside_x = far_first(x_near, "far")
    across_x = far_second(*beside_x, "far")
    dy_near = jnp.concatenate(gather(after(dy_mine, *beside_x), "far"))
    beside_dy = far_first(dy_near, "near")
    weights = lax.optimization_barrier((*weights, dy_near))[:RING]
    x_all = jnp.concatenate([x_near, beside_x[0], *across_x, beside_x[1]])
    weights = laid(weights, 0, b)
    gate_up, down = weights[:, : 2 * block_ff], weights[:, 2 * block_ff :]
    product = dot(x_all, gate_up, ((1,), (0,)))
    beside_dy, product = lax.optimization_barrier((beside_dy, product))
    across_dy = far_second(*beside_dy, "near")
    dy_all = jnp.concatenate([dy_near, beside_dy[0], *across_dy, beside_dy[1]])

    def over_features(product):
        parts = product.reshape(RING * RING, RING, owners * quarter, -1)
        return scatter([parts[:, k].reshape(-1, parts.shape[-1]) for k in range(RING)], "c")

    def of_all_rows(gathered):
        blocks = jnp.stack(gathered).reshape(RING, RING * RING, owners * quarter, -1)
        return blocks.transpose(1, 0, 2, 3).reshape(-1, blocks.shape[-1])

    def turned(own):
        return own.reshape(RING, RING, owners * quarter, -1).swapaxes(0, 1).reshape(own.shape)

    gate_up_own = over_features(product)
    gate, up = gate_up_own[:, :block_ff], gate_up_own[:, block_ff:]
    sig = jax.nn.sigmoid(gate)
    act = gate * sig
    hidden = (act * up).astype(BF16)
    dhidden = turned(over_features(dot(dy_all, down, ((1,), (0,)))))
    dup = (dhidden * act).astype(BF16)
    dgate = (dhidden * up * sig * (1.0 + gate * (1.0 - sig))).astype(BF16)
    both = gather(jnp.concatenate([dgate, dup], axis=1), "c")
    d_all = of_all_rows(both)

    count = d_all.shape[0] // RING
    dx = [dot(part, gate_up, ((1,), (1,))) for part in rows_of(d_all, count)]
    dx, arrived = ring_scatter(dx, "far")
    grads = dot(after(x_all, *arrived), d_all, ((0,), (0,))).astype(BF16)
    count = count // RING
    hidden_all = of_all_rows(gather(after(turned(hidden), *both[1:]), "c"))
    grad_down = after(dot(hidden_all, dy_all, ((0,), (0,))).astype(BF16), *arrived)
    grad_down = exchange([cut(grad_down, 1, b + k, block_d) for k in range(RING)], "b")
    grads = after(grads, *grad_down[1:])
    grads = [cut(grads, 0, b + k, block_d) for k in range(RING)]
    half = block_d // 2
    up = hop(jnp.concatenate([grads[1], grads[2][:half]]), "b", 1)
    low = hop(jnp.concatenate([grads[3], grads[2][half:]]), "b", -1)
    opposite = jnp.concatenate([hop(up[block_d:], "b", 1), hop(low[block_d:], "b", -1)])
    grads = [grads[0], low[:block_d], opposite, up[:block_d]]
    dx = scatter(rows_of(dx, count), "near").astype(BF16)
    parts = exchange(rows_of(dx, count // RING), "c")
    parts = laid([p[None] for p in parts], 0, c)
    back = []
    for k in range(RING):
        place = (x + k) % RING
        across_c = lax.dynamic_slice_in_dim(parts, place * block_d, block_d, 2)
        across_c = jnp.concatenate([across_c[j] for j in range(RING)], axis=1)
        back.append(jnp.where(core == 0, lax.dynamic_index_in_dim(parts, place, 0, keepdims=False), across_c))
    back = exchange(back, "x")
    back = laid([p.reshape(owners, 1, quarter, features) for p in back], 1, x).reshape(owners, capacity, features)
    returned = lax.all_to_all(after(back, *grads[1:]), "expert", split_axis=0, concat_axis=0, tiled=True)
    grad_tokens = jnp.einsum("esj,esd->jd", jnp.stack(placings), returned, preferred_element_type=F32)

    grad_down = laid(grad_down, 0, b)
    grad_gate = laid([g[:, :block_ff] for g in grads], 1, b)
    grad_up = laid([g[:, block_ff:] for g in grads], 1, b)
    return grad_tokens.astype(BF16), grad_gate[None], grad_up[None], grad_down[None]


def solution(mesh):
    owners, ring, batches = (mesh.shape[name] for name in ("expert", "etp", "edp"))
    grid = Mesh(mesh.devices.reshape(owners, ring, RING, batches // RING), DEVICES)
    tokens = ("expert", "z", "y")
    batch = ("z", "y")
    in_specs = (
        P(tokens, None),
        P(tokens, None),
        P(tokens, None),
        P("expert", batch, None),
        P("expert", batch, "etp"),
        P("expert", batch, "etp"),
        P("expert", "etp", batch),
    )
    out_specs = (
        P(tokens, "etp"),
        P("expert", batch, "etp"),
        P("expert", batch, "etp"),
        P("expert", "etp", batch),
    )
    return jax.shard_map(local, mesh=grid, in_specs=in_specs, out_specs=out_specs, check_vma=False)
```

```python
import jax
import jax.numpy as jnp
from jax import lax
from jax.sharding import Mesh
from jax.sharding import PartitionSpec as P

BF16 = jnp.bfloat16
F32 = jnp.float32
RING = 4
DEVICES = ("expert", "etp", "z", "y")
ROLES = {"x": ("etp", "etp"), "b": ("y", "z"), "c": ("z", "y"), "near": ("y", "etp"), "far": ("etp", "z")}


def hop(value, role, step):
    pairs = []
    for core, axis in enumerate(ROLES[role]):
        for place in range(RING**3):
            at = {"etp": place // RING**2, "z": place // RING % RING, "y": place % RING}
            at[axis] = (at[axis] + step) % RING
            target = (at["etp"] * RING + at["z"]) * RING + at["y"]
            pairs.append((core * RING**3 + place, core * RING**3 + target))
    return lax.ppermute(value, DEVICES, pairs)


def position(role):
    first, second = (lax.axis_index(axis) for axis in ROLES[role])
    return jnp.where(lax.axis_index("expert") == 0, first, second)


def beside(blocks, role):
    return hop(blocks[3], role, -1), hop(blocks[1], role, 1)


def across(blocks, role):
    return hop(blocks[2], role, 2)


def exchange(blocks, role):
    above, below = beside(blocks, role)
    return [blocks[0], above, across(blocks, role), below]


def gather(block, role):
    return exchange([block] * RING, role)


def scatter(parts, role):
    arrived = exchange([parts[0]] + [p.astype(BF16) for p in parts[1:]], role)
    return arrived[0] + arrived[1].astype(F32) + arrived[2].astype(F32) + arrived[3].astype(F32)


def far_first(block, role):
    return hop(block, role, -1), hop(block, role, 1)


def far_second(above, below, role):
    half = above.shape[0] // 2
    return hop(below[:half], role, 1), hop(above[half:], role, -1)


def ring_scatter(parts, role):
    half = parts[2].shape[0] // 2
    far = parts[2].astype(BF16)
    from_below = hop(far[:half], role, 1)
    from_above = hop(far[half:], role, -1)
    up = jnp.concatenate([parts[1][:half] + from_below.astype(F32), parts[1][half:]]).astype(BF16)
    down = jnp.concatenate([parts[3][:half], parts[3][half:] + from_above.astype(F32)]).astype(BF16)
    total = parts[0] + hop(up, role, 1).astype(F32) + hop(down, role, -1).astype(F32)
    return total, (from_below, from_above)


def cut(value, dim, place, size):
    return lax.dynamic_slice_in_dim(value, place % RING * size, size, dim)


def laid(blocks, dim, me):
    size = blocks[0].shape[dim]
    shape = list(blocks[0].shape)
    shape[dim] = size * RING
    whole = jnp.zeros(shape, blocks[0].dtype)
    for k, block in enumerate(blocks):
        whole = lax.dynamic_update_slice_in_dim(whole, block, (me + k) % RING * size, dim)
    return whole


def rows_of(value, count):
    return [value[k * count : (k + 1) * count] for k in range(RING)]


def after(value, *others):
    return lax.optimization_barrier((value, *others))[0]


def dot(a, b, dims):
    return lax.dot_general(a, b, (dims, ((), ())), preferred_element_type=F32)


def local(expert_ids, gate_prob, dout, stored_rows, w_gate, w_up, w_down):
    core, x, b, c = lax.axis_index("expert"), position("x"), position("b"), position("c")
    owners = 2
    tokens, width = dout.shape
    rows = stored_rows.shape[1]
    capacity = rows // owners
    quarter = capacity // RING
    features = width // RING
    block_ff = w_gate.shape[2] // RING
    block_d = w_gate.shape[1]

    def to_features(part):
        blocks = []
        for k in range(RING):
            place = (c + k) % RING
            starts = [jnp.where(core == 0, RING * place + j, RING * j + place) * block_d for j in range(RING)]
            blocks.append(jnp.concatenate([lax.dynamic_slice_in_dim(part, s, block_d, 1) for s in starts], axis=1))
        return jnp.concatenate(exchange(blocks, "c"))

    mine = stored_rows[0].reshape(owners, RING, quarter, width)
    mine = lax.dynamic_index_in_dim(mine, x, 1, keepdims=False).reshape(owners * quarter, width)
    x_mine = to_features(mine)
    x_near = jnp.concatenate(gather(x_mine, "near"))
    dout, expert_ids = after(dout, x_mine), after(expert_ids, x_mine)

    slots = lax.broadcasted_iota(jnp.int32, (capacity, tokens), 0)
    placings = []
    outgoing = []
    for expert in range(owners):
        named = expert_ids == expert
        chosen = jnp.any(named, axis=1)
        weight_row = jnp.sum(jnp.where(named, gate_prob, jnp.float32(0.0)), axis=1)
        rank = jnp.cumsum(chosen.astype(jnp.int32)) - 1
        placing = (chosen[None, :] & (rank[None, :] == slots)).astype(BF16)
        scaled = (weight_row[:, None] * dout.astype(F32)).astype(BF16)
        outgoing.append(dot(cut(placing, 0, x, quarter), scaled, ((1,), (0,))).astype(BF16))
        placings.append(placing)
    incoming = lax.all_to_all(jnp.stack(outgoing), "expert", split_axis=0, concat_axis=0, tiled=True)
    weights = jnp.concatenate([w_gate[0], w_up[0], w_down[0].T], axis=1).reshape(block_d, 3, RING, block_ff)
    weights = after(weights, x_mine)
    blocks = [lax.dynamic_index_in_dim(weights, (b + k) % RING, 2, keepdims=False) for k in range(RING)]
    blocks = [block.reshape(block_d, -1) for block in blocks]
    weights = exchange(blocks, "b")
    dy_mine = to_features(after(incoming, x_near).reshape(owners * quarter, width))
    beside_x = far_first(x_near, "far")
    across_x = far_second(*beside_x, "far")
    dy_near = jnp.concatenate(gather(after(dy_mine, *beside_x), "far"))
    beside_dy = far_first(dy_near, "near")
    weights = lax.optimization_barrier((*weights, dy_near))[:RING]
    x_all = jnp.concatenate([x_near, beside_x[0], *across_x, beside_x[1]])
    weights = laid(weights, 0, b)
    gate_up, down = weights[:, : 2 * block_ff], weights[:, 2 * block_ff :]
    def by_place(product):
        parts = product.reshape(RING * RING, RING, owners * quarter, -1)
        parts = [parts[:, k].reshape(-1, parts.shape[-1]) for k in range(RING)]
        return [parts[0]] + [p.astype(BF16) for p in parts[1:]]

    product = by_place(dot(x_all, gate_up, ((1,), (0,))))
    beside_dy, product = lax.optimization_barrier((beside_dy, product))
    across_dy = far_second(*beside_dy, "near")
    dy_all = jnp.concatenate([dy_near, beside_dy[0], *across_dy, beside_dy[1]])

    def of_all_rows(gathered):
        blocks = jnp.stack(gathered).reshape(RING, RING * RING, owners * quarter, -1)
        return blocks.transpose(1, 0, 2, 3).reshape(-1, blocks.shape[-1])

    def turned(own):
        return own.reshape(RING, RING, owners * quarter, -1).swapaxes(0, 1).reshape(own.shape)

    gate_up_own = scatter(product, "c")
    gate, up = gate_up_own[:, :block_ff], gate_up_own[:, block_ff:]
    sig = jax.nn.sigmoid(gate)
    act = gate * sig
    hidden = (act * up).astype(BF16)
    dhidden = turned(scatter(by_place(dot(dy_all, down, ((1,), (0,)))), "c"))
    dup = (dhidden * act).astype(BF16)
    dgate = (dhidden * up * sig * (1.0 + gate * (1.0 - sig))).astype(BF16)
    both = gather(jnp.concatenate([dgate, dup], axis=1), "c")
    d_all = of_all_rows(both)

    count = d_all.shape[0] // RING
    dx = [dot(part, gate_up, ((1,), (1,))) for part in rows_of(d_all, count)]
    dx, arrived = ring_scatter(dx, "far")
    grads = dot(after(x_all, *arrived), d_all, ((0,), (0,))).astype(BF16)
    count = count // RING
    hidden_all = of_all_rows(gather(after(turned(hidden), *both[1:]), "c"))
    grad_down = after(dot(hidden_all, dy_all, ((0,), (0,))).astype(BF16), *arrived)
    grad_down = exchange([cut(grad_down, 1, b + k, block_d) for k in range(RING)], "b")
    grads = after(grads, *grad_down[1:])
    grads = [cut(grads, 0, b + k, block_d) for k in range(RING)]
    half = block_d // 2
    up = hop(jnp.concatenate([grads[1], grads[2][:half]]), "b", 1)
    low = hop(jnp.concatenate([grads[3], grads[2][half:]]), "b", -1)
    opposite = jnp.concatenate([hop(up[block_d:], "b", 1), hop(low[block_d:], "b", -1)])
    grads = [grads[0], low[:block_d], opposite, up[:block_d]]
    dx = scatter(rows_of(dx, count), "near").astype(BF16)
    parts = exchange(rows_of(dx, count // RING), "c")
    parts = laid([p[None] for p in parts], 0, c)
    back = []
    for k in range(RING):
        place = (x + k) % RING
        across_c = lax.dynamic_slice_in_dim(parts, place * block_d, block_d, 2)
        across_c = jnp.concatenate([across_c[j] for j in range(RING)], axis=1)
        back.append(jnp.where(core == 0, lax.dynamic_index_in_dim(parts, place, 0, keepdims=False), across_c))
    back = exchange(back, "x")
    back = laid([p.reshape(owners, 1, quarter, features) for p in back], 1, x).reshape(owners, capacity, features)
    returned = lax.all_to_all(after(back, *grads[1:]), "expert", split_axis=0, concat_axis=0, tiled=True)
    grad_tokens = jnp.einsum("esj,esd->jd", jnp.stack(placings), returned, preferred_element_type=F32)

    grad_down = laid(grad_down, 0, b)
    grad_gate = laid([g[:, :block_ff] for g in grads], 1, b)
    grad_up = laid([g[:, block_ff:] for g in grads], 1, b)
    return grad_tokens.astype(BF16), grad_gate[None], grad_up[None], grad_down[None]


def solution(mesh):
    owners, ring, batches = (mesh.shape[name] for name in ("expert", "etp", "edp"))
    grid = Mesh(mesh.devices.reshape(owners, ring, RING, batches // RING), DEVICES)
    tokens = ("expert", "z", "y")
    batch = ("z", "y")
    in_specs = (
        P(tokens, None),
        P(tokens, None),
        P(tokens, None),
        P("expert", batch, None),
        P("expert", batch, "etp"),
        P("expert", batch, "etp"),
        P("expert", "etp", batch),
    )
    out_specs = (
        P(tokens, "etp"),
        P("expert", batch, "etp"),
        P("expert", batch, "etp"),
        P("expert", "etp", batch),
    )
    return jax.shard_map(local, mesh=grid, in_specs=in_specs, out_specs=out_specs, check_vma=False)
```
